32 devices in a mesh: chan: 16 (over z, y, x), facet: 2 (over core).
Axes of the slice: x: 2, y: 2, z: 4, core: 2. Of those that a mesh axis runs over, the one named last changes fastest.
Arguments:
- estimate: float32 [256, 128, 256], P('chan', None, 'facet'), may hold values from -6 to 6
- dirty: float32 [256, 128, 256], P('chan', None, 'facet'), may hold values from -6 to 6
- weights: float32 [256, 128, 256], P('chan', None, 'facet'), may hold values from 0.2 to 1
- margin: int32 [2], replicated, may hold values from 1 to 16, as said below
- blend_table: int32 [2, 160], replicated, may hold values from 1 to 8
- tau_steps: int32 [2], replicated, may hold values from 1 to 4
Outputs:
- updated: float32 [256, 128, 256], P('chan', None, 'facet')
The draws below stay inside these ranges and needn't reach their ends.
Inputs may be any that keep to these rules, and one draw needn't show every extreme that they name: Some facet has margin exactly 16.
All inputs are finite; a program needn't handle non-finite values.
Results may differ from the reference program's by a relative error of at most 0.00012.
Values sent between devices are 32-bit elements; how exact they have to be, the bound alone decides.
A program may use at most 64 MiB of HBM per device.

```python
import math
import jax
import jax.numpy as jnp
from jax import lax

C = 256
W = 128
HD = 128
OV = 16
NS_STEPS = 2
ITERS = 2
FACETS = 2
H = 256


def draw_margin(key, part):
    first_key = jax.random.fold_in(key, 11)
    second_key = jax.random.fold_in(key, 23)
    widths = jax.random.randint(first_key, (FACETS,), 1, OV + 1)
    chosen = jax.random.randint(second_key, (), 0, FACETS)
    return jnp.where(jnp.arange(FACETS) == chosen, OV, widths).astype(jnp.int32)


def plant(result, own_key, low, largest):
    index_at = [jax.random.randint(jax.random.fold_in(own_key, axis), (), 0, length) for axis, length in enumerate(result.shape)]
    longest = result.shape.index(max(result.shape))
    next_to = index_at[:longest] + [(index_at[longest] + 1) % result.shape[longest]] + index_at[longest + 1:]
    return result.at[tuple(index_at)].set(low).at[tuple(next_to)].set(largest)


def raised(values, rng, source, target, shards_of, factor):
    owner, partner = [(jnp.arange(values.shape[dim]) // (values.shape[dim] // shards_of)).reshape([-1 if axis == dim else 1 for axis in range(values.ndim)]) for dim in (source, target)]
    chosen = jax.random.permutation(rng, shards_of)[partner]
    strong = (owner == chosen) | (owner == (partner + shards_of // 2) % shards_of)
    return jnp.where(strong, factor * values, values)


def level_of(key, shape, shards, smallest, high):
    def one(dim, blocks):
        steps = jax.random.uniform(jax.random.fold_in(jax.random.fold_in(key, 6), dim), (blocks,), jnp.float32, smallest / len(shards), high / len(shards))
        return jnp.repeat(jnp.exp(steps), shape[dim] // blocks).reshape((-1,) + (1,) * (len(shape) - dim - 1))

    loudness = one(*shards[0])
    for cut in shards[1:]:
        loudness = loudness * one(*cut)
    return loudness


def heavy_noise(rng, shape, spread, most, pieces, heavy, kind=jnp.bfloat16):
    entries = spread * jax.random.normal(rng, shape, jnp.float32)
    if pieces:
        entries = entries * level_of(rng, shape, pieces, -0.22, 0.18)
    return jnp.clip(raised(entries, jax.random.fold_in(rng, 3), *heavy), -most, most).astype(kind)


def setup_inputs(seed: int = 0) -> dict:
    splits = jax.random.split(jax.random.key(seed), 7)
    estimate = heavy_noise(splits[0], (C, W, H), 1.0, 6.0, ((0, 16), (2, 2)), (1, 0, 16, 2.0), jnp.float32)
    dirty = heavy_noise(splits[1], (C, W, H), 1.0, 6.0, ((0, 16), (2, 2)), (2, 0, 16, 2.0), jnp.float32)
    weights = jnp.clip(jnp.exp(math.log(1.0) - 1.609438 * jax.random.uniform(splits[2], (C, W, H), jnp.float32) ** level_of(splits[2], (C, W, H), ((0, 16), (2, 2)), -0.2, 0.2)), 0.2, 1.0)
    margin = draw_margin(jax.random.fold_in(splits[6], 71), 0)
    blend_table = plant(jax.random.randint(splits[4], (FACETS, HD + 2 * OV), 1, 9), jax.random.fold_in(splits[4], 1), 1, 8).astype(jnp.int32)
    tau_steps = jax.random.randint(splits[5], (ITERS,), 1, 5).astype(jnp.int32)
    return {"estimate": estimate, "dirty": dirty, "weights": weights, "margin": margin, "blend_table": blend_table, "tau_steps": tau_steps}


def apply_shrink(gram, columns, tau_value):
    channel_count = gram.shape[0]
    identity = jnp.eye(channel_count, dtype=jnp.float32)
    mean_eigen = jnp.trace(gram) / channel_count + 1e-06
    target = (gram + 0.01 * mean_eigen * identity) / (16.16 * mean_eigen)
    inverse_root = identity
    for newton_step in range(NS_STEPS):
        middle = 1.5 * identity - 0.5 * jnp.dot(inverse_root, target, precision=lax.Precision.HIGHEST)
        target = jnp.dot(target, middle, precision=lax.Precision.HIGHEST)
        inverse_root = jnp.dot(middle, inverse_root, precision=lax.Precision.HIGHEST)
    factor = 0.1 * tau_value / math.sqrt(1.01)
    kernel = identity - factor * inverse_root
    return jnp.dot(kernel, columns, precision=lax.Precision.HIGHEST)

def reference(estimate, dirty, weights, margin, blend_table, tau_steps):
    channel_count, image_width, height = estimate.shape
    center = HD
    ext_len = center + 2 * OV
    row_index = jnp.arange(ext_len, dtype=jnp.int32)
    current = estimate
    for iteration in range(ITERS):
        tau_value = tau_steps[iteration].astype(jnp.float32)
        moved_cube = current - weights * (current - dirty)
        padded = jnp.pad(moved_cube, ((0, 0), (0, 0), (OV, OV)))
        numerator = jnp.zeros_like(padded)
        denominator = jnp.zeros((height + 2 * OV,), jnp.float32)
        for facet_index in range(FACETS):
            width_here = margin[facet_index]
            row_mask = ((row_index >= OV - width_here) & (row_index < center + OV + width_here)).astype(jnp.float32)
            first_row = facet_index * center
            block = padded[:, :, first_row:first_row + ext_len] * row_mask
            columns = block.reshape(channel_count, -1)
            gram = jnp.dot(columns, columns.T, precision=lax.Precision.HIGHEST)
            shrunk = apply_shrink(gram, columns, tau_value).reshape(block.shape)
            row_weight = blend_table[facet_index].astype(jnp.float32) * row_mask
            numerator = numerator.at[:, :, first_row:first_row + ext_len].add(shrunk * row_weight)
            denominator = denominator.at[first_row:first_row + ext_len].add(row_weight)
        current = numerator[:, :, OV:OV + height] / denominator[OV:OV + height]
    return current
```

```python
import functools
import math

import jax
import jax.numpy as jnp
from jax import lax
from jax.experimental import pallas as pl
from jax.experimental.pallas import tpu as pltpu
from jax.sharding import PartitionSpec as P

OV = 16
NS_STEPS = 2
ITERS = 2
MESH = pl.DeviceIdType.MESH
HIGHEST = lax.Precision.HIGHEST
F32 = jnp.float32


def dot(a, b):
    return jnp.dot(a, b, precision=HIGHEST, preferred_element_type=F32)


def dot_nt(a, b):
    return lax.dot_general(
        a, b, (((1,), (1,)), ((), ())), precision=HIGHEST, preferred_element_type=F32
    )


def kernel(
    n, facets, est, dirty, wts, margin, table, tau, out,
    send, recv, cube, gram, kmat, g_part, g_parts, g_sum, g_all,
    halo_out, halo_in, rim, back_out, back_in,
    send_sem, recv_sem, g_send_sem, g_recv_sem, h_send_sem, h_recv_sem,
):
    me = lax.axis_index("chan")
    f = lax.axis_index("facet")
    _, wl, c_loc, rows = out.shape
    total = n * c_loc
    has = (f > 0, f < facets - 1)
    near = (f - 1, f + 1)

    def peers(body):
        def step(s, carry):
            body(lax.rem(me + s, n))
            return carry

        lax.fori_loop(1, n, step, 0)

    def over_columns(body):
        def step(w, carry):
            body(w)
            return carry

        lax.fori_loop(0, wl, step, 0)

    barrier = pltpu.get_barrier_semaphore()
    peers(lambda j: pl.semaphore_signal(barrier, inc=1, device_id={"chan": j}, device_id_type=MESH))
    for s in range(2):
        @pl.when(has[s])
        def _():
            pl.semaphore_signal(
                barrier, inc=1, device_id={"facet": near[s]}, device_id_type=MESH
            )
    sides = lax.min(f, 1) + lax.min(facets - 1 - f, 1)
    pl.semaphore_wait(barrier, n - 1 + sides)

    ext = table.shape[1]
    weights_of = table[...].astype(F32)
    row_of = lax.broadcasted_iota(jnp.int32, (facets, 1), 0)
    e_of = lax.broadcasted_iota(jnp.int32, (ext, rows), 0)
    l_of = lax.broadcasted_iota(jnp.int32, (ext, rows), 1)
    lane = lax.broadcasted_iota(jnp.int32, (1, rows), 1)
    packed = lax.rem(lane, OV)
    packed_of = lax.rem(l_of, OV)

    def facet_row(g, place):
        row = jnp.sum(jnp.where(row_of == g, weights_of, 0.0), axis=0, keepdims=True)
        row = jnp.broadcast_to(row, (8, ext))
        pick = jnp.where(e_of == place, 1.0, 0.0)
        return dot(row, pick)[0:1]

    own_margin = margin[f]
    before_margin = margin[lax.max(f - 1, 0)]
    after_margin = margin[lax.min(f + 1, facets - 1)]
    core_weight = facet_row(f, l_of + OV)
    before_part = facet_row(f - 1, l_of + (rows + OV))
    after_part = facet_row(f + 1, l_of - (rows - OV))
    before_ok = jnp.where((lane < before_margin) & (f > 0), 1.0, 0.0)
    after_ok = jnp.where((lane >= rows - after_margin) & (f < facets - 1), 1.0, 0.0)
    inverse = 1.0 / (core_weight + before_part * before_ok + after_part * after_ok)
    used = jnp.where(lane < wl * OV, 1.0, 0.0)
    rim_mask = (
        jnp.where(packed >= OV - own_margin, 1.0, 0.0) * used,
        jnp.where(packed < own_margin, 1.0, 0.0) * used,
    )
    rim_weight = (
        facet_row(f, packed_of) * rim_mask[0],
        facet_row(f, packed_of + (rows + OV)) * rim_mask[1],
    )

    def block_copy(k, j, landing):
        return pltpu.make_async_remote_copy(
            src_ref=send.at[k, j],
            dst_ref=landing,
            send_sem=send_sem.at[k, j],
            recv_sem=recv_sem.at[k, me],
            device_id={"chan": j},
            device_id_type=MESH,
        )

    def block_wait(k, j, landing):
        pltpu.make_async_remote_copy(
            src_ref=send.at[k, j],
            dst_ref=landing,
            send_sem=send_sem.at[k, j],
            recv_sem=recv_sem.at[k, j],
            device_id={"chan": j},
            device_id_type=MESH,
        ).wait_recv()

    def turned(value):
        return jnp.swapaxes(value, 0, 1)

    def send_moved(j):
        value = est[:, j]
        send[0, j] = turned(value - wts[:, j] * (value - dirty[:, j]))
        block_copy(0, j, recv.at[0, me]).start()

    def send_weights(j):
        send[1, j] = turned(wts[:, j])
        block_copy(1, j, recv.at[1, me]).start()

    peers(send_moved)
    peers(send_weights)

    def stage_dirty(j):
        send[2, j] = turned(dirty[:, j])

    peers(stage_dirty)
    mine = est[:, me]
    recv[0, me] = turned(mine - wts[:, me] * (mine - dirty[:, me]))
    recv[1, me] = turned(wts[:, me])
    recv[2, me] = turned(dirty[:, me])

    def send_dirty(first, last):
        def step(s, carry):
            block_copy(2, lax.rem(me + s, n), recv.at[2, me]).start()
            return carry

        lax.fori_loop(first, last, step, 0)

    half = n // 2

    peers(lambda j: block_wait(0, j, recv.at[0, j]))

    def matrix(k, w):
        return recv[k, :, w].reshape(total, rows)

    def side_copy(it, what, src, dst, s, there):
        return pltpu.make_async_remote_copy(
            src_ref=src.at[it, s],
            dst_ref=dst.at[it, there],
            send_sem=h_send_sem.at[it, what, s],
            recv_sem=h_recv_sem.at[it, what, there],
            device_id={"facet": near[s]},
            device_id_type=MESH,
        )

    eye = jnp.where(
        lax.broadcasted_iota(jnp.int32, (total, total), 0)
        == lax.broadcasted_iota(jnp.int32, (total, total), 1),
        1.0,
        0.0,
    )

    for it in range(ITERS):
        for s in range(2):
            @pl.when(has[s])
            def _():
                low = 0 if s == 0 else rows - OV
                block = jnp.zeros((total, rows), F32)
                for w in range(wl):
                    rolled = pltpu.roll(matrix(0, w), (w * OV - low) % rows, 1)
                    block = jnp.where(lane // OV == w, rolled, block)
                halo_out[it, s] = block
                side_copy(it, 0, halo_out, halo_in, s, 1 - s).start()

        gram[...] = jnp.zeros((total, total), F32)

        def add_gram(w):
            m = matrix(0, w)
            gram[...] += dot_nt(m, m)

        over_columns(add_gram)
        for s in range(2):
            @pl.when(has[s])
            def _():
                side_copy(it, 0, halo_out, halo_in, s, s).wait_recv()
                m = halo_in[it, s] * rim_mask[s]
                rim[s] = m
                gram[...] += dot_nt(m, m)

        g_part[it] = gram[...].reshape(n, c_loc, total)

        def g_copy(what, src, dst, j, sem_at):
            return pltpu.make_async_remote_copy(
                src_ref=src,
                dst_ref=dst,
                send_sem=g_send_sem.at[it, what, j],
                recv_sem=g_recv_sem.at[it, what, sem_at],
                device_id={"chan": j},
                device_id_type=MESH,
            )

        peers(lambda j: g_copy(0, g_part.at[it, j], g_parts.at[it, me], j, me).start())
        g_parts[it, me] = g_part[it, me]
        if it == 0:
            send_dirty(1, half)
        peers(lambda j: g_copy(0, g_part.at[it, j], g_parts.at[it, j], j, j).wait_recv())
        g_sum[it] = jnp.sum(g_parts[it], axis=0)
        peers(lambda j: g_copy(1, g_sum.at[it], g_all.at[it, me], j, me).start())
        g_all[it, me] = g_sum[it]
        if it == 0:
            send_dirty(half, n)
        peers(lambda j: g_copy(1, g_sum.at[it], g_all.at[it, j], j, j).wait_recv())

        full = g_all[it].reshape(total, total)
        mean = jnp.sum(full * eye) / total + 1e-06
        target = (full + (0.01 * mean) * eye) / (16.16 * mean)
        middle = 1.5 * eye - 0.5 * target
        root = middle
        for _step in range(NS_STEPS - 1):
            target = dot(target, middle)
            middle = 1.5 * eye - 0.5 * dot(root, target)
            root = dot(middle, root)
        factor = (0.1 / math.sqrt(1.01)) * tau[it].astype(F32)
        kmat[...] = eye - factor * root

        for s in range(2):
            @pl.when(has[s])
            def _():
                back_out[it, s] = dot(kmat[...], rim[s]) * rim_weight[s]
                side_copy(it, 1, back_out, back_in, s, 1 - s).start()

        def shrink(w):
            value = dot(kmat[...], matrix(0, w)) * (core_weight * inverse)
            cube[:, w] = value.reshape(n, c_loc, rows)

        over_columns(shrink)
        for s in range(2):
            @pl.when(has[s])
            def _():
                side_copy(it, 1, back_out, back_in, s, s).wait_recv()
                low = 0 if s == 0 else rows - OV
                inside = (lane >= low) & (lane < low + OV)
                extra = back_in[it, s]
                for w in range(wl):
                    rolled = pltpu.roll(extra, (low - w * OV) % rows, 1)
                    piece = jnp.where(inside, rolled * inverse, 0.0)
                    cube[:, w] += piece.reshape(n, c_loc, rows)

        if it < ITERS - 1:
            if it == 0:
                peers(lambda j: block_wait(1, j, recv.at[1, j]))
                peers(lambda j: block_wait(2, j, recv.at[2, j]))

            def move(w):
                value = cube[:, w]
                recv[0, :, w] = value - recv[1, :, w] * (value - recv[2, :, w])

            over_columns(move)

    def final_copy(j, landing, sem_at):
        return pltpu.make_async_remote_copy(
            src_ref=cube.at[j],
            dst_ref=landing,
            send_sem=send_sem.at[3, j],
            recv_sem=recv_sem.at[3, sem_at],
            device_id={"chan": j},
            device_id_type=MESH,
        )

    peers(lambda j: final_copy(j, out.at[me], me).start())
    out[me] = cube[me]

    def drain(j):
        for k in range(3):
            block_copy(k, j, recv.at[k, me]).wait_send()
        for it in range(ITERS):
            for what in range(2):
                src = g_part.at[it, j] if what == 0 else g_sum.at[it]
                dst = g_parts.at[it, me] if what == 0 else g_all.at[it, me]
                pltpu.make_async_remote_copy(
                    src_ref=src,
                    dst_ref=dst,
                    send_sem=g_send_sem.at[it, what, j],
                    recv_sem=g_recv_sem.at[it, what, me],
                    device_id={"chan": j},
                    device_id_type=MESH,
                ).wait_send()

    peers(drain)
    for s in range(2):
        @pl.when(has[s])
        def _():
            for it in range(ITERS):
                side_copy(it, 0, halo_out, halo_in, s, 1 - s).wait_send()
                side_copy(it, 1, back_out, back_in, s, 1 - s).wait_send()
    peers(lambda j: final_copy(j, out.at[j], j).wait_recv())
    peers(lambda j: final_copy(j, out.at[me], me).wait_send())


def per_device(n, facets, estimate, dirty, weights, margin, blend_table, tau_steps):
    c_loc, width, rows = estimate.shape
    wl = width // n
    total = n * c_loc
    cut = lambda a: a.reshape(c_loc, n, wl, rows)
    vmem = pl.BlockSpec(memory_space=pltpu.VMEM)
    smem = pl.BlockSpec(memory_space=pltpu.SMEM)
    dma = pltpu.SemaphoreType.DMA
    result = pl.pallas_call(
        functools.partial(kernel, n, facets),
        out_shape=jax.ShapeDtypeStruct((n, wl, c_loc, rows), F32),
        in_specs=[vmem, vmem, vmem, smem, vmem, smem],
        out_specs=vmem,
        scratch_shapes=[
            pltpu.VMEM((3, n, wl, c_loc, rows), F32),
            pltpu.VMEM((3, n, wl, c_loc, rows), F32),
            pltpu.VMEM((n, wl, c_loc, rows), F32),
            pltpu.VMEM((total, total), F32),
            pltpu.VMEM((total, total), F32),
            pltpu.VMEM((ITERS, n, c_loc, total), F32),
            pltpu.VMEM((ITERS, n, c_loc, total), F32),
            pltpu.VMEM((ITERS, c_loc, total), F32),
            pltpu.VMEM((ITERS, n, c_loc, total), F32),
            pltpu.VMEM((ITERS, 2, total, rows), F32),
            pltpu.VMEM((ITERS, 2, total, rows), F32),
            pltpu.VMEM((2, total, rows), F32),
            pltpu.VMEM((ITERS, 2, total, rows), F32),
            pltpu.VMEM((ITERS, 2, total, rows), F32),
            dma((4, n)),
            dma((4, n)),
            dma((ITERS, 2, n)),
            dma((ITERS, 2, n)),
            dma((ITERS, 2, 2)),
            dma((ITERS, 2, 2)),
        ],
        compiler_params=pltpu.CompilerParams(
            collective_id=0, has_side_effects=True, vmem_limit_bytes=48 * 1024 * 1024
        ),
        cost_estimate=pl.CostEstimate(
            flops=ITERS * 4 * total * total * wl * (rows + 2 * OV),
            bytes_accessed=16 * c_loc * width * rows,
            transcendentals=0,
        ),
        name="denoise",
    )(cut(estimate), cut(dirty), cut(weights), margin, blend_table, tau_steps)
    return result.transpose(2, 0, 1, 3).reshape(c_loc, width, rows)


def solution(mesh):
    n, facets = mesh.shape["chan"], mesh.shape["facet"]
    cube = P("chan", None, "facet")
    return jax.shard_map(
        functools.partial(per_device, n, facets),
        mesh=mesh,
        in_specs=(cube, cube, cube, P(), P(), P()),
        out_specs=cube,
        check_vma=False,
    )
```

```python
import functools
import math

import jax
import jax.numpy as jnp
from jax import lax
from jax.experimental import pallas as pl
from jax.experimental.pallas import tpu as pltpu
from jax.sharding import PartitionSpec as P

OV = 16
NS_STEPS = 2
ITERS = 2
MESH = pl.DeviceIdType.MESH
F32 = jnp.float32
BF16 = jnp.bfloat16


def dot(a, b):
    return jnp.dot(a, b, preferred_element_type=F32)


def dot_nt(a, b):
    return lax.dot_general(a, b, (((1,), (1,)), ((), ())), preferred_element_type=F32)


def split(value):
    high = value.astype(BF16)
    return high, (value - high.astype(F32)).astype(BF16)


def dot_split(a, b):
    return dot(a[0], b[0]) + (dot(a[0], b[1]) + dot(a[1], b[0]))


def kernel(
    n, facets, est_hbm, dirty_hbm, wts_hbm, margin, table, tau, out,
    est, dirty, wts, send, recv, cube, high, low, gram, g_part, g_parts, g_sum, g_all,
    halo_out, halo_in, rim, back_out, back_in,
    in_sem, send_sem, recv_sem, g_send_sem, g_recv_sem, h_send_sem, h_recv_sem,
):
    me = lax.axis_index("chan")
    f = lax.axis_index("facet")
    _, wl, c_loc, rows = out.shape
    total = n * c_loc
    has = (f > 0, f < facets - 1)
    near = (f - 1, f + 1)
    half = n // 2
    upper, place = me // half, lax.rem(me, half)

    def peers(body):
        def step(t, carry):
            other = lax.rem(place + t, half)
            body((1 - upper) * half + other)
            body(upper * half + other)
            return carry

        body((1 - upper) * half + place)
        lax.fori_loop(1, half, step, 0)

    loads = [
        pltpu.make_async_copy(src, dst, in_sem.at[i])
        for i, (src, dst) in enumerate(((est_hbm, est), (dirty_hbm, dirty), (wts_hbm, wts)))
    ]
    for load in loads:
        load.start()

    barrier = pltpu.get_barrier_semaphore()
    peers(lambda j: pl.semaphore_signal(barrier, inc=1, device_id={"chan": j}, device_id_type=MESH))
    for s in range(2):
        @pl.when(has[s])
        def _():
            pl.semaphore_signal(
                barrier, inc=1, device_id={"facet": near[s]}, device_id_type=MESH
            )
    sides = lax.min(f, 1) + lax.min(facets - 1 - f, 1)
    pl.semaphore_wait(barrier, n - 1 + sides)
    for load in loads:
        load.wait()

    cut = wl // 2
    sets = ((0, 0, wl), (1, 0, wl), (2, 0, cut), (2, cut, wl - cut))

    def block_copy(q, j, origin, sem_at):
        k, first, count = sets[q]
        return pltpu.make_async_remote_copy(
            src_ref=send.at[k, j, pl.ds(first, count)],
            dst_ref=recv.at[k, origin, pl.ds(first, count)],
            send_sem=send_sem.at[q, j],
            recv_sem=recv_sem.at[q, sem_at],
            device_id={"chan": j},
            device_id_type=MESH,
        )

    def block_send(q):
        peers(lambda j: block_copy(q, j, me, me).start())

    def block_wait(q):
        peers(lambda j: block_copy(q, j, j, j).wait_recv())

    def turned(value):
        return jnp.swapaxes(value, 0, 1)

    def send_moved(j):
        value = est[:, j]
        send[0, j] = turned(value - wts[:, j] * (value - dirty[:, j]))
        block_copy(0, j, me, me).start()

    def send_weights(j):
        send[1, j] = turned(wts[:, j])
        block_copy(1, j, me, me).start()

    def stage_dirty(j):
        send[2, j] = turned(dirty[:, j])

    peers(send_moved)
    peers(send_weights)
    peers(stage_dirty)
    mine = est[:, me]
    recv[0, me] = turned(mine - wts[:, me] * (mine - dirty[:, me]))
    recv[1, me] = turned(wts[:, me])
    recv[2, me] = turned(dirty[:, me])

    ext = table.shape[1]
    weights_of = table[...].astype(F32)
    row_of = lax.broadcasted_iota(jnp.int32, (facets, 1), 0)
    e_of = lax.broadcasted_iota(jnp.int32, (ext, rows), 0)
    l_of = lax.broadcasted_iota(jnp.int32, (ext, rows), 1)
    lane = lax.broadcasted_iota(jnp.int32, (1, rows), 1)
    packed = lax.rem(lane, OV)
    packed_of = lax.rem(l_of, OV)

    def facet_row(g, where):
        row = jnp.sum(jnp.where(row_of == g, weights_of, 0.0), axis=0, keepdims=True)
        row = jnp.broadcast_to(row, (16, ext)).astype(BF16)
        pick = jnp.where(e_of == where, 1.0, 0.0).astype(BF16)
        return dot(row, pick)[0:1]

    own_margin = margin[f]
    before_margin = margin[lax.max(f - 1, 0)]
    after_margin = margin[lax.min(f + 1, facets - 1)]
    core_weight = facet_row(f, l_of + OV)
    before_part = facet_row(f - 1, l_of + (rows + OV))
    after_part = facet_row(f + 1, l_of - (rows - OV))
    before_ok = jnp.where((lane < before_margin) & (f > 0), 1.0, 0.0)
    after_ok = jnp.where((lane >= rows - after_margin) & (f < facets - 1), 1.0, 0.0)
    inverse = 1.0 / (core_weight + before_part * before_ok + after_part * after_ok)
    used = jnp.where(lane < wl * OV, 1.0, 0.0)
    rim_mask = (
        jnp.where(packed >= OV - own_margin, 1.0, 0.0) * used,
        jnp.where(packed < own_margin, 1.0, 0.0) * used,
    )
    rim_weight = (
        facet_row(f, packed_of) * rim_mask[0],
        facet_row(f, packed_of + (rows + OV)) * rim_mask[1],
    )
    eye = jnp.where(
        lax.broadcasted_iota(jnp.int32, (total, total), 0)
        == lax.broadcasted_iota(jnp.int32, (total, total), 1),
        1.0,
        0.0,
    )

    def block(first, count=1):
        return slice(first * rows, (first + count) * rows)

    def matrix(k, w):
        return recv[k, :, w].reshape(total, rows)

    def put(at, value):
        high[:, block(at)], low[:, block(at)] = split(value)

    def add_gram(first, count, fresh):
        h, l = high[:, block(first, count)], low[:, block(first, count)]
        same, cross = dot_nt(h, h), dot_nt(h, l)
        if fresh:
            gram[0], gram[1] = same, cross
        else:
            gram[0] += same
            gram[1] += cross

    high[:, block(wl, 2)] = jnp.zeros((total, 2 * rows), BF16)
    low[:, block(wl, 2)] = jnp.zeros((total, 2 * rows), BF16)

    def side_copy(it, what, src, dst, s, there):
        return pltpu.make_async_remote_copy(
            src_ref=src.at[it, s],
            dst_ref=dst.at[it, there],
            send_sem=h_send_sem.at[it, what, s],
            recv_sem=h_recv_sem.at[it, what, there],
            device_id={"facet": near[s]},
            device_id_type=MESH,
        )

    def scatter_copy(it, j, origin, sem_at):
        return pltpu.make_async_remote_copy(
            src_ref=g_part.at[it, j],
            dst_ref=g_parts.at[it, origin],
            send_sem=g_send_sem.at[it, 0, j],
            recv_sem=g_recv_sem.at[it, 0, sem_at],
            device_id={"chan": j},
            device_id_type=MESH,
        )

    def gather_copy(it, j, origin, sem_at):
        return pltpu.make_async_remote_copy(
            src_ref=g_sum.at[it],
            dst_ref=g_all.at[it, origin],
            send_sem=g_send_sem.at[it, 1, j],
            recv_sem=g_recv_sem.at[it, 1, sem_at],
            device_id={"chan": j},
            device_id_type=MESH,
        )

    def final_copy(j, landing, sem_at):
        return pltpu.make_async_remote_copy(
            src_ref=cube.at[j],
            dst_ref=landing,
            send_sem=send_sem.at[4, j],
            recv_sem=recv_sem.at[4, sem_at],
            device_id={"chan": j},
            device_id_type=MESH,
        )

    block_wait(0)
    hc = total // 2
    for it in range(ITERS):
        for s in range(2):
            @pl.when(has[s])
            def _():
                start = 0 if s == 0 else rows - OV
                rows_out = jnp.zeros((total, rows), F32)
                for w in range(wl):
                    rolled = pltpu.roll(matrix(0, w), (w * OV - start) % rows, 1)
                    rows_out = jnp.where(lane // OV == w, rolled, rows_out)
                halo_out[it, s] = rows_out
                side_copy(it, 0, halo_out, halo_in, s, 1 - s).start()

        if it == 0:
            for w in range(wl):
                put(w, matrix(0, w))
            add_gram(0, wl, True)
        else:
            add_gram(cut, wl - cut, False)
        for s in range(2):
            @pl.when(has[s])
            def _():
                side_copy(it, 0, halo_out, halo_in, s, s).wait_recv()
                m = halo_in[it, s] * rim_mask[s]
                rim[s] = m
                put(wl + s, m)
        add_gram(wl, 2, False)

        cross = gram[1]
        whole = gram[0] + (cross + cross.T)
        blocks = jnp.concatenate([whole[:hc, :hc], whole[hc:, :hc], whole[hc:, hc:]], axis=0)
        g_part[it] = blocks.reshape(g_part.shape[1:])
        peers(lambda j: scatter_copy(it, j, me, me).start())
        g_parts[it, me] = g_part[it, me]
        if it == 0:
            block_send(2)
        peers(lambda j: scatter_copy(it, j, j, j).wait_recv())
        g_sum[it] = jnp.sum(g_parts[it], axis=0)
        peers(lambda j: gather_copy(it, j, me, me).start())
        g_all[it, me] = g_sum[it]
        if it == 0:
            block_send(3)
        peers(lambda j: gather_copy(it, j, j, j).wait_recv())

        blocks = g_all[it].reshape(3 * hc, hc)
        top, corner, end = blocks[:hc], blocks[hc : 2 * hc], blocks[2 * hc :]
        full = jnp.concatenate(
            [jnp.concatenate([top, corner.T], axis=1), jnp.concatenate([corner, end], axis=1)],
            axis=0,
        )
        mean = jnp.sum(full * eye) / total + 1e-06
        target = (full + (0.01 * mean) * eye) / (16.16 * mean)
        middle = 1.5 * eye - 0.5 * target
        root = middle
        for _step in range(NS_STEPS - 1):
            target = dot_split(split(target), split(middle))
            middle = 1.5 * eye - 0.5 * dot_split(split(root), split(target))
            root = dot_split(split(middle), split(root))
        factor = (0.1 / math.sqrt(1.01)) * tau[it].astype(F32)
        taken = split(factor * root)

        def product(first, count):
            at = block(first, count)
            return dot_split(taken, (high[:, at], low[:, at]))

        for s in range(2):
            @pl.when(has[s])
            def _():
                back_out[it, s] = (rim[s] - product(wl + s, 1)) * rim_weight[s]
                side_copy(it, 1, back_out, back_in, s, 1 - s).start()

        scale = core_weight * inverse
        for w in range(0, wl, 2):
            less = product(w, 2)
            for i in range(2):
                value = (matrix(0, w + i) - less[:, block(i)]) * scale
                cube[:, w + i] = value.reshape(n, c_loc, rows)
        for s in range(2):
            @pl.when(has[s])
            def _():
                side_copy(it, 1, back_out, back_in, s, s).wait_recv()
                start = 0 if s == 0 else rows - OV
                inside = (lane >= start) & (lane < start + OV)
                extra = back_in[it, s]
                for w in range(wl):
                    rolled = pltpu.roll(extra, (start - w * OV) % rows, 1)
                    piece = jnp.where(inside, rolled * inverse, 0.0)
                    cube[:, w] += piece.reshape(n, c_loc, rows)

        if it < ITERS - 1:
            def move(w):
                value = cube[:, w]
                value = value - recv[1, :, w] * (value - recv[2, :, w])
                recv[0, :, w] = value
                put(w, value.reshape(total, rows))

            if it == 0:
                block_wait(1)
                block_wait(2)
            for w in range(cut):
                move(w)
            add_gram(0, cut, True)
            if it == 0:
                block_wait(3)
            for w in range(cut, wl):
                move(w)

    peers(lambda j: final_copy(j, out.at[me], me).start())
    out[me] = cube[me]

    def drain(j):
        for q in range(len(sets)):
            block_copy(q, j, me, me).wait_send()
        for it in range(ITERS):
            scatter_copy(it, j, me, me).wait_send()
            gather_copy(it, j, me, me).wait_send()

    peers(drain)
    for s in range(2):
        @pl.when(has[s])
        def _():
            for it in range(ITERS):
                side_copy(it, 0, halo_out, halo_in, s, 1 - s).wait_send()
                side_copy(it, 1, back_out, back_in, s, 1 - s).wait_send()
    peers(lambda j: final_copy(j, out.at[j], j).wait_recv())
    peers(lambda j: final_copy(j, out.at[me], me).wait_send())


def per_device(n, facets, estimate, dirty, weights, margin, blend_table, tau_steps):
    c_loc, width, rows = estimate.shape
    wl = width // n
    total = n * c_loc
    piece = 3 * total // (2 * n)
    cut = lambda a: a.reshape(c_loc, n, wl, rows)
    vmem = pl.BlockSpec(memory_space=pltpu.VMEM)
    hbm = pl.BlockSpec(memory_space=pltpu.HBM)
    smem = pl.BlockSpec(memory_space=pltpu.SMEM)
    dma = pltpu.SemaphoreType.DMA
    result = pl.pallas_call(
        functools.partial(kernel, n, facets),
        out_shape=jax.ShapeDtypeStruct((n, wl, c_loc, rows), F32),
        in_specs=[hbm, hbm, hbm, smem, vmem, smem],
        out_specs=vmem,
        scratch_shapes=[
            pltpu.VMEM((c_loc, n, wl, rows), F32),
            pltpu.VMEM((c_loc, n, wl, rows), F32),
            pltpu.VMEM((c_loc, n, wl, rows), F32),
            pltpu.VMEM((3, n, wl, c_loc, rows), F32),
            pltpu.VMEM((3, n, wl, c_loc, rows), F32),
            pltpu.VMEM((n, wl, c_loc, rows), F32),
            pltpu.VMEM((total, (wl + 2) * rows), BF16),
            pltpu.VMEM((total, (wl + 2) * rows), BF16),
            pltpu.VMEM((2, total, total), F32),
            pltpu.VMEM((ITERS, n, piece, total // 2), F32),
            pltpu.VMEM((ITERS, n, piece, total // 2), F32),
            pltpu.VMEM((ITERS, piece, total // 2), F32),
            pltpu.VMEM((ITERS, n, piece, total // 2), F32),
            pltpu.VMEM((ITERS, 2, total, rows), F32),
            pltpu.VMEM((ITERS, 2, total, rows), F32),
            pltpu.VMEM((2, total, rows), F32),
            pltpu.VMEM((ITERS, 2, total, rows), F32),
            pltpu.VMEM((ITERS, 2, total, rows), F32),
            dma((3,)),
            dma((5, n)),
            dma((5, n)),
            dma((ITERS, 2, n)),
            dma((ITERS, 2, n)),
            dma((ITERS, 2, 2)),
            dma((ITERS, 2, 2)),
        ],
        compiler_params=pltpu.CompilerParams(
            collective_id=0, has_side_effects=True, vmem_limit_bytes=48 * 1024 * 1024
        ),
        cost_estimate=pl.CostEstimate(
            flops=ITERS * 4 * total * total * wl * (rows + 2 * OV),
            bytes_accessed=16 * c_loc * width * rows,
            transcendentals=0,
        ),
        name="denoise",
    )(cut(estimate), cut(dirty), cut(weights), margin, blend_table, tau_steps)
    return result.transpose(2, 0, 1, 3).reshape(c_loc, width, rows)


def solution(mesh):
    n, facets = mesh.shape["chan"], mesh.shape["facet"]
    cube = P("chan", None, "facet")
    return jax.shard_map(
        functools.partial(per_device, n, facets),
        mesh=mesh,
        in_specs=(cube, cube, cube, P(), P(), P()),
        out_specs=cube,
        check_vma=False,
    )
```

```python
import functools
import math

import jax
import jax.numpy as jnp
from jax import lax
from jax.experimental import pallas as pl
from jax.experimental.pallas import tpu as pltpu
from jax.sharding import PartitionSpec as P

OV = 16
NS_STEPS = 2
ITERS = 2
MESH = pl.DeviceIdType.MESH
F32 = jnp.float32
BF16 = jnp.bfloat16


def dot(a, b):
    return jnp.dot(a, b, preferred_element_type=F32)


def dot_nt(a, b):
    return lax.dot_general(a, b, (((1,), (1,)), ((), ())), preferred_element_type=F32)


def split(value):
    high = value.astype(BF16)
    return high, (value - high.astype(F32)).astype(BF16)


def dot_split(a, b):
    return dot(a[0], b[0]) + (dot(a[0], b[1]) + dot(a[1], b[0]))


def kernel(
    n, facets, est_hbm, dirty_hbm, wts_hbm, margin, table, tau, out,
    est, dirty, wts, send, recv, cube, high, low, gram, g_part, g_parts, g_half, g_pair, g_sum, g_all,
    halo_out, halo_in, rim, back_out, back_in,
    in_sem, send_sem, recv_sem, g_send_sem, g_recv_sem, p_send_sem, p_recv_sem, h_send_sem, h_recv_sem,
):
    me = lax.axis_index("chan")
    f = lax.axis_index("facet")
    _, wl, c_loc, rows = out.shape
    total = n * c_loc
    has = (f > 0, f < facets - 1)
    near = (f - 1, f + 1)
    half = n // 2
    upper, place = me // half, lax.rem(me, half)
    mirror = (1 - upper) * half + place

    def peers(body):
        def step(t, carry):
            other = lax.rem(place + t, half)
            body((1 - upper) * half + other)
            body(upper * half + other)
            return carry

        body(mirror)
        lax.fori_loop(1, half, step, 0)

    def inside_half(body):
        def step(t, carry):
            body(lax.rem(place + t, half))
            return carry

        lax.fori_loop(1, half, step, 0)

    loads = [
        pltpu.make_async_copy(src, dst, in_sem.at[i])
        for i, (src, dst) in enumerate(((est_hbm, est), (dirty_hbm, dirty), (wts_hbm, wts)))
    ]
    for load in loads:
        load.start()

    barrier = pltpu.get_barrier_semaphore()
    peers(lambda j: pl.semaphore_signal(barrier, inc=1, device_id={"chan": j}, device_id_type=MESH))
    for s in range(2):
        @pl.when(has[s])
        def _():
            pl.semaphore_signal(
                barrier, inc=1, device_id={"facet": near[s]}, device_id_type=MESH
            )
    sides = lax.min(f, 1) + lax.min(facets - 1 - f, 1)
    pl.semaphore_wait(barrier, n - 1 + sides)
    for load in loads:
        load.wait()

    cut = wl // 2
    halves = ((0, cut), (cut, wl - cut))
    sets = ((0, 0, wl),) + tuple((k, *h) for k in (1, 2) for h in halves)

    def block_copy(q, j, origin, sem_at):
        k, first, count = sets[q]
        return pltpu.make_async_remote_copy(
            src_ref=send.at[k, j, pl.ds(first, count)],
            dst_ref=recv.at[k, origin, pl.ds(first, count)],
            send_sem=send_sem.at[q, j],
            recv_sem=recv_sem.at[q, sem_at],
            device_id={"chan": j},
            device_id_type=MESH,
        )

    def block_send(q):
        peers(lambda j: block_copy(q, j, me, me).start())

    def block_wait(q):
        peers(lambda j: block_copy(q, j, j, j).wait_recv())

    def turned(value):
        return jnp.swapaxes(value, 0, 1)

    def send_moved(j):
        value = est[:, j]
        send[0, j] = turned(value - wts[:, j] * (value - dirty[:, j]))
        block_copy(0, j, me, me).start()

    def send_weights(j):
        send[1, j] = turned(wts[:, j])
        block_copy(1, j, me, me).start()

    def stage_dirty(j):
        send[2, j] = turned(dirty[:, j])

    peers(send_moved)
    peers(send_weights)
    peers(stage_dirty)
    mine = est[:, me]
    recv[0, me] = turned(mine - wts[:, me] * (mine - dirty[:, me]))
    recv[1, me] = turned(wts[:, me])
    recv[2, me] = turned(dirty[:, me])

    ext = table.shape[1]
    weights_of = table[...].astype(F32)
    row_of = lax.broadcasted_iota(jnp.int32, (facets, 1), 0)
    e_of = lax.broadcasted_iota(jnp.int32, (ext, rows), 0)
    l_of = lax.broadcasted_iota(jnp.int32, (ext, rows), 1)
    lane = lax.broadcasted_iota(jnp.int32, (1, rows), 1)
    packed = lax.rem(lane, OV)
    packed_of = lax.rem(l_of, OV)

    def facet_row(g, where):
        row = jnp.sum(jnp.where(row_of == g, weights_of, 0.0), axis=0, keepdims=True)
        row = jnp.broadcast_to(row, (16, ext)).astype(BF16)
        pick = jnp.where(e_of == where, 1.0, 0.0).astype(BF16)
        return dot(row, pick)[0:1]

    own_margin = margin[f]
    before_margin = margin[lax.max(f - 1, 0)]
    after_margin = margin[lax.min(f + 1, facets - 1)]
    core_weight = facet_row(f, l_of + OV)
    before_part = facet_row(f - 1, l_of + (rows + OV))
    after_part = facet_row(f + 1, l_of - (rows - OV))
    before_ok = jnp.where((lane < before_margin) & (f > 0), 1.0, 0.0)
    after_ok = jnp.where((lane >= rows - after_margin) & (f < facets - 1), 1.0, 0.0)
    inverse = 1.0 / (core_weight + before_part * before_ok + after_part * after_ok)
    used = jnp.where(lane < wl * OV, 1.0, 0.0)
    rim_mask = (
        jnp.where(packed >= OV - own_margin, 1.0, 0.0) * used,
        jnp.where(packed < own_margin, 1.0, 0.0) * used,
    )
    rim_weight = (
        facet_row(f, packed_of) * rim_mask[0],
        facet_row(f, packed_of + (rows + OV)) * rim_mask[1],
    )
    eye = jnp.where(
        lax.broadcasted_iota(jnp.int32, (total, total), 0)
        == lax.broadcasted_iota(jnp.int32, (total, total), 1),
        1.0,
        0.0,
    )

    def block(first, count=1):
        return slice(first * rows, (first + count) * rows)

    def matrix(k, w):
        return recv[k, :, w].reshape(total, rows)

    def put(at, value):
        high[:, block(at)], low[:, block(at)] = split(value)

    def add_gram(first, count, fresh):
        h, l = high[:, block(first, count)], low[:, block(first, count)]
        same, cross = dot_nt(h, h), dot_nt(h, l)
        if fresh:
            gram[0], gram[1] = same, cross
        else:
            gram[0] += same
            gram[1] += cross

    high[:, block(wl, 2)] = jnp.zeros((total, 2 * rows), BF16)
    low[:, block(wl, 2)] = jnp.zeros((total, 2 * rows), BF16)

    def side_copy(it, what, src, dst, s, there):
        return pltpu.make_async_remote_copy(
            src_ref=src.at[it, s],
            dst_ref=dst.at[it, there],
            send_sem=h_send_sem.at[it, what, s],
            recv_sem=h_recv_sem.at[it, what, there],
            device_id={"facet": near[s]},
            device_id_type=MESH,
        )

    def scatter_copy(it, p, origin, sem_at):
        return pltpu.make_async_remote_copy(
            src_ref=g_part.at[it, p],
            dst_ref=g_parts.at[it, origin],
            send_sem=g_send_sem.at[it, 0, p],
            recv_sem=g_recv_sem.at[it, 0, sem_at],
            device_id={"chan": upper * half + p},
            device_id_type=MESH,
        )

    def gather_copy(it, p, origin, sem_at):
        return pltpu.make_async_remote_copy(
            src_ref=g_sum.at[it],
            dst_ref=g_all.at[it, origin],
            send_sem=g_send_sem.at[it, 1, p],
            recv_sem=g_recv_sem.at[it, 1, sem_at],
            device_id={"chan": upper * half + p},
            device_id_type=MESH,
        )

    def pair_copy(it):
        return pltpu.make_async_remote_copy(
            src_ref=g_half.at[it],
            dst_ref=g_pair.at[it],
            send_sem=p_send_sem.at[it],
            recv_sem=p_recv_sem.at[it],
            device_id={"chan": mirror},
            device_id_type=MESH,
        )

    def final_copy(h, j, origin, sem_at):
        first, count = halves[h]
        return pltpu.make_async_remote_copy(
            src_ref=cube.at[j, pl.ds(first, count)],
            dst_ref=out.at[origin, pl.ds(first, count)],
            send_sem=send_sem.at[5 + h, j],
            recv_sem=recv_sem.at[5 + h, sem_at],
            device_id={"chan": j},
            device_id_type=MESH,
        )

    block_wait(0)
    hc = total // 2
    for it in range(ITERS):
        for s in range(2):
            @pl.when(has[s])
            def _():
                start = 0 if s == 0 else rows - OV
                rows_out = jnp.zeros((total, rows), F32)
                for w in range(wl):
                    rolled = pltpu.roll(matrix(0, w), (w * OV - start) % rows, 1)
                    rows_out = jnp.where(lane // OV == w, rolled, rows_out)
                halo_out[it, s] = rows_out
                side_copy(it, 0, halo_out, halo_in, s, 1 - s).start()

        if it == 0:
            for w in range(wl):
                put(w, matrix(0, w))
            add_gram(0, wl, True)
        else:
            add_gram(cut, wl - cut, False)
        for s in range(2):
            @pl.when(has[s])
            def _():
                side_copy(it, 0, halo_out, halo_in, s, s).wait_recv()
                m = halo_in[it, s] * rim_mask[s]
                rim[s] = m
                put(wl + s, m)
        add_gram(wl, 2, False)

        cross = gram[1]
        whole = gram[0] + (cross + cross.T)
        blocks = jnp.concatenate([whole[:hc, :hc], whole[hc:, :hc], whole[hc:, hc:]], axis=0)
        g_part[it] = blocks.reshape(g_part.shape[1:])
        inside_half(lambda p: scatter_copy(it, p, place, place).start())
        g_parts[it, place] = g_part[it, place]
        if it == 0:
            block_send(2)
        inside_half(lambda p: scatter_copy(it, p, p, p).wait_recv())
        g_half[it] = jnp.sum(g_parts[it], axis=0)
        pair_copy(it).start()
        if it == 0:
            block_send(3)
        pair_copy(it).wait_recv()
        g_sum[it] = g_half[it] + g_pair[it]
        inside_half(lambda p: gather_copy(it, p, place, place).start())
        g_all[it, place] = g_sum[it]
        if it == 0:
            block_send(4)
        inside_half(lambda p: gather_copy(it, p, p, p).wait_recv())

        blocks = g_all[it].reshape(3 * hc, hc)
        top, corner, end = blocks[:hc], blocks[hc : 2 * hc], blocks[2 * hc :]
        full = jnp.concatenate(
            [jnp.concatenate([top, corner.T], axis=1), jnp.concatenate([corner, end], axis=1)],
            axis=0,
        )
        mean = jnp.sum(full * eye) / total + 1e-06
        target = (full + (0.01 * mean) * eye) / (16.16 * mean)
        middle = 1.5 * eye - 0.5 * target
        root = middle
        for _step in range(NS_STEPS - 1):
            target = dot_split(split(target), split(middle))
            middle = 1.5 * eye - 0.5 * dot_split(split(root), split(target))
            root = dot_split(split(middle), split(root))
        factor = (0.1 / math.sqrt(1.01)) * tau[it].astype(F32)
        taken = split(factor * root)

        def product(first, count):
            at = block(first, count)
            return dot_split(taken, (high[:, at], low[:, at]))

        for s in range(2):
            @pl.when(has[s])
            def _():
                back_out[it, s] = (rim[s] - product(wl + s, 1)) * rim_weight[s]
                side_copy(it, 1, back_out, back_in, s, 1 - s).start()

        scale = core_weight * inverse
        step = 2 - cut % 2
        for h, (first, count) in enumerate(halves):
            for w in range(first, first + count, step):
                less = product(w, step)
                for i in range(step):
                    value = (matrix(0, w + i) - less[:, block(i)]) * scale
                    cube[:, w + i] = value.reshape(n, c_loc, rows)
            for s in range(2):
                @pl.when(has[s])
                def _():
                    if h == 0:
                        side_copy(it, 1, back_out, back_in, s, s).wait_recv()
                    start = 0 if s == 0 else rows - OV
                    inside = (lane >= start) & (lane < start + OV)
                    extra = back_in[it, s]
                    for w in range(first, first + count):
                        rolled = pltpu.roll(extra, (start - w * OV) % rows, 1)
                        piece = jnp.where(inside, rolled * inverse, 0.0)
                        cube[:, w] += piece.reshape(n, c_loc, rows)
            if it == ITERS - 1:
                peers(lambda j: final_copy(h, j, me, me).start())

        if it < ITERS - 1:
            def move(w):
                value = cube[:, w]
                value = value - recv[1, :, w] * (value - recv[2, :, w])
                recv[0, :, w] = value
                put(w, value.reshape(total, rows))

            for h, (first, count) in enumerate(halves):
                if it == 0:
                    block_wait(1 + h)
                    block_wait(3 + h)
                for w in range(first, first + count):
                    move(w)
                if h == 0:
                    add_gram(first, count, True)

    out[me] = cube[me]

    def drain(j):
        for q in range(len(sets)):
            block_copy(q, j, me, me).wait_send()

    def drain_half(p):
        for it in range(ITERS):
            scatter_copy(it, p, place, place).wait_send()
            gather_copy(it, p, place, place).wait_send()

    peers(drain)
    inside_half(drain_half)
    for it in range(ITERS):
        pair_copy(it).wait_send()
    for s in range(2):
        @pl.when(has[s])
        def _():
            for it in range(ITERS):
                side_copy(it, 0, halo_out, halo_in, s, 1 - s).wait_send()
                side_copy(it, 1, back_out, back_in, s, 1 - s).wait_send()
    for h in range(2):
        peers(lambda j: final_copy(h, j, j, j).wait_recv())
    for h in range(2):
        peers(lambda j: final_copy(h, j, me, me).wait_send())


def per_device(n, facets, estimate, dirty, weights, margin, blend_table, tau_steps):
    c_loc, width, rows = estimate.shape
    wl = width // n
    total = n * c_loc
    half = n // 2
    piece = 3 * total // n
    cut = lambda a: a.reshape(c_loc, n, wl, rows)
    vmem = pl.BlockSpec(memory_space=pltpu.VMEM)
    hbm = pl.BlockSpec(memory_space=pltpu.HBM)
    smem = pl.BlockSpec(memory_space=pltpu.SMEM)
    dma = pltpu.SemaphoreType.DMA
    result = pl.pallas_call(
        functools.partial(kernel, n, facets),
        out_shape=jax.ShapeDtypeStruct((n, wl, c_loc, rows), F32),
        in_specs=[hbm, hbm, hbm, smem, vmem, smem],
        out_specs=vmem,
        scratch_shapes=[
            pltpu.VMEM((c_loc, n, wl, rows), F32),
            pltpu.VMEM((c_loc, n, wl, rows), F32),
            pltpu.VMEM((c_loc, n, wl, rows), F32),
            pltpu.VMEM((3, n, wl, c_loc, rows), F32),
            pltpu.VMEM((3, n, wl, c_loc, rows), F32),
            pltpu.VMEM((n, wl, c_loc, rows), F32),
            pltpu.VMEM((total, (wl + 2) * rows), BF16),
            pltpu.VMEM((total, (wl + 2) * rows), BF16),
            pltpu.VMEM((2, total, total), F32),
            pltpu.VMEM((ITERS, half, piece, total // 2), F32),
            pltpu.VMEM((ITERS, half, piece, total // 2), F32),
            pltpu.VMEM((ITERS, piece, total // 2), F32),
            pltpu.VMEM((ITERS, piece, total // 2), F32),
            pltpu.VMEM((ITERS, piece, total // 2), F32),
            pltpu.VMEM((ITERS, half, piece, total // 2), F32),
            pltpu.VMEM((ITERS, 2, total, rows), F32),
            pltpu.VMEM((ITERS, 2, total, rows), F32),
            pltpu.VMEM((2, total, rows), F32),
            pltpu.VMEM((ITERS, 2, total, rows), F32),
            pltpu.VMEM((ITERS, 2, total, rows), F32),
            dma((3,)),
            dma((7, n)),
            dma((7, n)),
            dma((ITERS, 2, half)),
            dma((ITERS, 2, half)),
            dma((ITERS,)),
            dma((ITERS,)),
            dma((ITERS, 2, 2)),
            dma((ITERS, 2, 2)),
        ],
        compiler_params=pltpu.CompilerParams(
            collective_id=0, has_side_effects=True, vmem_limit_bytes=127 * 1024 * 1024 // 2
        ),
        cost_estimate=pl.CostEstimate(
            flops=ITERS * 4 * total * total * wl * (rows + 2 * OV),
            bytes_accessed=16 * c_loc * width * rows,
            transcendentals=0,
        ),
        name="denoise",
    )(cut(estimate), cut(dirty), cut(weights), margin, blend_table, tau_steps)
    return result.transpose(2, 0, 1, 3).reshape(c_loc, width, rows)


def solution(mesh):
    n, facets = mesh.shape["chan"], mesh.shape["facet"]
    cube = P("chan", None, "facet")
    return jax.shard_map(
        functools.partial(per_device, n, facets),
        mesh=mesh,
        in_specs=(cube, cube, cube, P(), P(), P()),
        out_specs=cube,
        check_vma=False,
    )
```

```python
import functools
import math

import jax
import jax.numpy as jnp
from jax import lax
from jax.experimental import pallas as pl
from jax.experimental.pallas import tpu as pltpu
from jax.sharding import PartitionSpec as P

OV = 16
NS_STEPS = 2
ITERS = 2
MESH = pl.DeviceIdType.MESH
F32 = jnp.float32
BF16 = jnp.bfloat16


def dot(a, b):
    return jnp.dot(a, b, preferred_element_type=F32)


def dot_nt(a, b):
    return lax.dot_general(a, b, (((1,), (1,)), ((), ())), preferred_element_type=F32)


def split(value):
    high = value.astype(BF16)
    return high, (value - high.astype(F32)).astype(BF16)


def dot_split(a, b):
    return dot(a[0], b[0]) + (dot(a[0], b[1]) + dot(a[1], b[0]))


def kernel(
    n, facets, est_hbm, dirty_hbm, wts_hbm, margin, table, tau, out,
    est, dirty, wts, send, recv, cube, high, low, gram, g_part, g_parts, g_half, g_pair, g_sum, g_all,
    halo_out, halo_in, rim, back_out, back_in,
    in_sem, send_sem, recv_sem, g_send_sem, g_recv_sem, p_send_sem, p_recv_sem, h_send_sem, h_recv_sem,
):
    me = lax.axis_index("chan")
    f = lax.axis_index("facet")
    _, wl, c_loc, rows = out.shape
    total = n * c_loc
    has = (f > 0, f < facets - 1)
    near = (f - 1, f + 1)
    half = n // 2
    upper, place = me // half, lax.rem(me, half)
    mirror = (1 - upper) * half + place

    def peers(body):
        def step(t, carry):
            other = lax.rem(place + t, half)
            body((1 - upper) * half + other)
            body(upper * half + other)
            return carry

        body(mirror)
        lax.fori_loop(1, half, step, 0)

    def inside_half(body):
        def step(t, carry):
            body(lax.rem(place + t, half))
            return carry

        lax.fori_loop(1, half, step, 0)

    loads = [
        pltpu.make_async_copy(src, dst, in_sem.at[i])
        for i, (src, dst) in enumerate(((est_hbm, est), (dirty_hbm, dirty), (wts_hbm, wts)))
    ]
    for load in loads:
        load.start()

    barrier = pltpu.get_barrier_semaphore()
    peers(lambda j: pl.semaphore_signal(barrier, inc=1, device_id={"chan": j}, device_id_type=MESH))
    for s in range(2):
        @pl.when(has[s])
        def _():
            pl.semaphore_signal(
                barrier, inc=1, device_id={"facet": near[s]}, device_id_type=MESH
            )
    sides = lax.min(f, 1) + lax.min(facets - 1 - f, 1)
    pl.semaphore_wait(barrier, n - 1 + sides)
    for load in loads:
        load.wait()

    part = max(1, wl // 4)
    tail = wl - part
    pieces = ((0, tail), (tail, part))
    final_pieces = ((0, part), (part, tail))
    dirty_pieces = [c for c in ((0, part), (part, tail - part), (tail, part)) if c[1] > 0]
    sets = [(0, 0, wl)] + [(1, *c) for c in pieces] + [(2, *c) for c in dirty_pieces]

    def block_copy(q, j, origin, sem_at):
        k, first, count = sets[q]
        return pltpu.make_async_remote_copy(
            src_ref=send.at[k, j, pl.ds(first, count)],
            dst_ref=recv.at[k, origin, pl.ds(first, count)],
            send_sem=send_sem.at[q, j],
            recv_sem=recv_sem.at[q, sem_at],
            device_id={"chan": j},
            device_id_type=MESH,
        )

    def block_send(q):
        peers(lambda j: block_copy(q, j, me, me).start())

    def block_wait(q):
        peers(lambda j: block_copy(q, j, j, j).wait_recv())

    def turned(value):
        return jnp.swapaxes(value, 0, 1)

    def send_moved(j):
        value = est[:, j]
        send[0, j] = turned(value - wts[:, j] * (value - dirty[:, j]))
        block_copy(0, j, me, me).start()

    def send_weights(j):
        send[1, j] = turned(wts[:, j])
        block_copy(1, j, me, me).start()

    def stage_dirty(j):
        send[2, j] = turned(dirty[:, j])

    peers(send_moved)
    peers(send_weights)
    peers(stage_dirty)
    mine = est[:, me]
    recv[0, me] = turned(mine - wts[:, me] * (mine - dirty[:, me]))
    recv[1, me] = turned(wts[:, me])
    recv[2, me] = turned(dirty[:, me])

    ext = table.shape[1]
    weights_of = table[...].astype(F32)
    row_of = lax.broadcasted_iota(jnp.int32, (facets, 1), 0)
    e_of = lax.broadcasted_iota(jnp.int32, (ext, rows), 0)
    l_of = lax.broadcasted_iota(jnp.int32, (ext, rows), 1)
    lane = lax.broadcasted_iota(jnp.int32, (1, rows), 1)
    packed = lax.rem(lane, OV)
    packed_of = lax.rem(l_of, OV)

    def facet_row(g, where):
        row = jnp.sum(jnp.where(row_of == g, weights_of, 0.0), axis=0, keepdims=True)
        row = jnp.broadcast_to(row, (16, ext)).astype(BF16)
        pick = jnp.where(e_of == where, 1.0, 0.0).astype(BF16)
        return dot(row, pick)[0:1]

    own_margin = margin[f]
    before_margin = margin[lax.max(f - 1, 0)]
    after_margin = margin[lax.min(f + 1, facets - 1)]
    core_weight = facet_row(f, l_of + OV)
    before_part = facet_row(f - 1, l_of + (rows + OV))
    after_part = facet_row(f + 1, l_of - (rows - OV))
    before_ok = jnp.where((lane < before_margin) & (f > 0), 1.0, 0.0)
    after_ok = jnp.where((lane >= rows - after_margin) & (f < facets - 1), 1.0, 0.0)
    inverse = 1.0 / (core_weight + before_part * before_ok + after_part * after_ok)
    used = jnp.where(lane < wl * OV, 1.0, 0.0)
    rim_mask = (
        jnp.where(packed >= OV - own_margin, 1.0, 0.0) * used,
        jnp.where(packed < own_margin, 1.0, 0.0) * used,
    )
    rim_weight = (
        facet_row(f, packed_of) * rim_mask[0],
        facet_row(f, packed_of + (rows + OV)) * rim_mask[1],
    )
    eye = jnp.where(
        lax.broadcasted_iota(jnp.int32, (total, total), 0)
        == lax.broadcasted_iota(jnp.int32, (total, total), 1),
        1.0,
        0.0,
    )

    def block(first, count=1):
        return slice(first * rows, (first + count) * rows)

    def matrix(k, w):
        return recv[k, :, w].reshape(total, rows)

    def put(at, value):
        high[:, block(at)], low[:, block(at)] = split(value)

    def add_gram(first, count, fresh):
        h, l = high[:, block(first, count)], low[:, block(first, count)]
        same, cross = dot_nt(h, h), dot_nt(h, l)
        if fresh:
            gram[0], gram[1] = same, cross
        else:
            gram[0] += same
            gram[1] += cross

    high[:, block(wl, 2)] = jnp.zeros((total, 2 * rows), BF16)
    low[:, block(wl, 2)] = jnp.zeros((total, 2 * rows), BF16)

    def side_copy(it, what, src, dst, s, there):
        return pltpu.make_async_remote_copy(
            src_ref=src.at[it, s],
            dst_ref=dst.at[it, there],
            send_sem=h_send_sem.at[it, what, s],
            recv_sem=h_recv_sem.at[it, what, there],
            device_id={"facet": near[s]},
            device_id_type=MESH,
        )

    def scatter_copy(it, p, origin, sem_at):
        return pltpu.make_async_remote_copy(
            src_ref=g_part.at[it, p],
            dst_ref=g_parts.at[it, origin],
            send_sem=g_send_sem.at[it, 0, p],
            recv_sem=g_recv_sem.at[it, 0, sem_at],
            device_id={"chan": upper * half + p},
            device_id_type=MESH,
        )

    def gather_copy(it, p, origin, sem_at):
        return pltpu.make_async_remote_copy(
            src_ref=g_sum.at[it],
            dst_ref=g_all.at[it, origin],
            send_sem=g_send_sem.at[it, 1, p],
            recv_sem=g_recv_sem.at[it, 1, sem_at],
            device_id={"chan": upper * half + p},
            device_id_type=MESH,
        )

    def pair_copy(it):
        return pltpu.make_async_remote_copy(
            src_ref=g_half.at[it],
            dst_ref=g_pair.at[it],
            send_sem=p_send_sem.at[it],
            recv_sem=p_recv_sem.at[it],
            device_id={"chan": mirror},
            device_id_type=MESH,
        )

    def final_copy(h, j, origin, sem_at):
        first, count = final_pieces[h]
        return pltpu.make_async_remote_copy(
            src_ref=cube.at[j, pl.ds(first, count)],
            dst_ref=out.at[origin, pl.ds(first, count)],
            send_sem=send_sem.at[len(sets) + h, j],
            recv_sem=recv_sem.at[len(sets) + h, sem_at],
            device_id={"chan": j},
            device_id_type=MESH,
        )

    block_wait(0)
    hc = total // 2
    for it in range(ITERS):
        for s in range(2):
            @pl.when(has[s])
            def _():
                start = 0 if s == 0 else rows - OV
                rows_out = jnp.zeros((total, rows), F32)
                for w in range(wl):
                    rolled = pltpu.roll(matrix(0, w), (w * OV - start) % rows, 1)
                    rows_out = jnp.where(lane // OV == w, rolled, rows_out)
                halo_out[it, s] = rows_out
                side_copy(it, 0, halo_out, halo_in, s, 1 - s).start()

        if it == 0:
            for w in range(wl):
                put(w, matrix(0, w))
            add_gram(0, wl, True)
        else:
            add_gram(tail, part, False)
        for s in range(2):
            @pl.when(has[s])
            def _():
                side_copy(it, 0, halo_out, halo_in, s, s).wait_recv()
                m = halo_in[it, s] * rim_mask[s]
                rim[s] = m
                put(wl + s, m)
        add_gram(wl, 2, False)

        cross = gram[1]
        whole = gram[0] + (cross + cross.T)
        blocks = jnp.concatenate([whole[:hc, :hc], whole[hc:, :hc], whole[hc:, hc:]], axis=0)
        g_part[it] = blocks.reshape(g_part.shape[1:])
        inside_half(lambda p: scatter_copy(it, p, place, place).start())
        g_parts[it, place] = g_part[it, place]
        if it == 0:
            block_send(2)
        inside_half(lambda p: scatter_copy(it, p, p, p).wait_recv())
        g_half[it] = jnp.sum(g_parts[it], axis=0)
        pair_copy(it).start()
        if it == 0:
            block_send(3)
        pair_copy(it).wait_recv()
        g_sum[it] = g_half[it] + g_pair[it]
        inside_half(lambda p: gather_copy(it, p, place, place).start())
        g_all[it, place] = g_sum[it]
        if it == 0:
            for q in range(4, len(sets)):
                block_send(q)
        inside_half(lambda p: gather_copy(it, p, p, p).wait_recv())

        blocks = g_all[it].reshape(3 * hc, hc)
        top, corner, end = blocks[:hc], blocks[hc : 2 * hc], blocks[2 * hc :]
        full = jnp.concatenate(
            [jnp.concatenate([top, corner.T], axis=1), jnp.concatenate([corner, end], axis=1)],
            axis=0,
        )
        mean = jnp.sum(full * eye) / total + 1e-06
        target = (full + (0.01 * mean) * eye) / (16.16 * mean)
        middle = 1.5 * eye - 0.5 * target
        root = middle
        for _step in range(NS_STEPS - 1):
            target = dot_split(split(target), split(middle))
            middle = 1.5 * eye - 0.5 * dot_split(split(root), split(target))
            root = dot_split(split(middle), split(root))
        factor = (0.1 / math.sqrt(1.01)) * tau[it].astype(F32)
        taken = split(factor * root)

        def product(first, count):
            at = block(first, count)
            return dot_split(taken, (high[:, at], low[:, at]))

        for s in range(2):
            @pl.when(has[s])
            def _():
                back_out[it, s] = (rim[s] - product(wl + s, 1)) * rim_weight[s]
                side_copy(it, 1, back_out, back_in, s, 1 - s).start()

        scale = core_weight * inverse
        step = 2 - part % 2
        for h, (first, count) in enumerate(final_pieces):
            for w in range(first, first + count, step):
                less = product(w, step)
                for i in range(step):
                    value = (matrix(0, w + i) - less[:, block(i)]) * scale
                    cube[:, w + i] = value.reshape(n, c_loc, rows)
            for s in range(2):
                @pl.when(has[s])
                def _():
                    if h == 0:
                        side_copy(it, 1, back_out, back_in, s, s).wait_recv()
                    start = 0 if s == 0 else rows - OV
                    inside = (lane >= start) & (lane < start + OV)
                    extra = back_in[it, s]
                    for w in range(first, first + count):
                        rolled = pltpu.roll(extra, (start - w * OV) % rows, 1)
                        piece = jnp.where(inside, rolled * inverse, 0.0)
                        cube[:, w] += piece.reshape(n, c_loc, rows)
            if it == ITERS - 1:
                peers(lambda j: final_copy(h, j, me, me).start())

        if it < ITERS - 1:
            def move(w):
                value = cube[:, w]
                value = value - recv[1, :, w] * (value - recv[2, :, w])
                recv[0, :, w] = value
                put(w, value.reshape(total, rows))

            for h, (first, count) in enumerate(pieces):
                if it == 0:
                    block_wait(1 + h)
                    for q in range(3, len(sets) - 1) if h == 0 else (len(sets) - 1,):
                        block_wait(q)
                for w in range(first, first + count):
                    move(w)
                if h == 0:
                    add_gram(first, count, True)

    own = pltpu.make_async_copy(cube.at[me], out.at[me], in_sem.at[3])
    own.start()

    def drain(j):
        for q in range(len(sets)):
            block_copy(q, j, me, me).wait_send()

    def drain_half(p):
        for it in range(ITERS):
            scatter_copy(it, p, place, place).wait_send()
            gather_copy(it, p, place, place).wait_send()

    peers(drain)
    inside_half(drain_half)
    for it in range(ITERS):
        pair_copy(it).wait_send()
    for s in range(2):
        @pl.when(has[s])
        def _():
            for it in range(ITERS):
                side_copy(it, 0, halo_out, halo_in, s, 1 - s).wait_send()
                side_copy(it, 1, back_out, back_in, s, 1 - s).wait_send()
    own.wait()
    for h in range(2):
        peers(lambda j: final_copy(h, j, j, j).wait_recv())
    for h in range(2):
        peers(lambda j: final_copy(h, j, me, me).wait_send())


def per_device(n, facets, estimate, dirty, weights, margin, blend_table, tau_steps):
    c_loc, width, rows = estimate.shape
    wl = width // n
    total = n * c_loc
    half = n // 2
    piece = 3 * total // n
    cut = lambda a: a.reshape(c_loc, n, wl, rows)
    vmem = pl.BlockSpec(memory_space=pltpu.VMEM)
    hbm = pl.BlockSpec(memory_space=pltpu.HBM)
    smem = pl.BlockSpec(memory_space=pltpu.SMEM)
    dma = pltpu.SemaphoreType.DMA
    result = pl.pallas_call(
        functools.partial(kernel, n, facets),
        out_shape=jax.ShapeDtypeStruct((n, wl, c_loc, rows), F32),
        in_specs=[hbm, hbm, hbm, smem, vmem, smem],
        out_specs=hbm,
        scratch_shapes=[
            pltpu.VMEM((c_loc, n, wl, rows), F32),
            pltpu.VMEM((c_loc, n, wl, rows), F32),
            pltpu.VMEM((c_loc, n, wl, rows), F32),
            pltpu.VMEM((3, n, wl, c_loc, rows), F32),
            pltpu.VMEM((3, n, wl, c_loc, rows), F32),
            pltpu.VMEM((n, wl, c_loc, rows), F32),
            pltpu.VMEM((total, (wl + 2) * rows), BF16),
            pltpu.VMEM((total, (wl + 2) * rows), BF16),
            pltpu.VMEM((2, total, total), F32),
            pltpu.VMEM((ITERS, half, piece, total // 2), F32),
            pltpu.VMEM((ITERS, half, piece, total // 2), F32),
            pltpu.VMEM((ITERS, piece, total // 2), F32),
            pltpu.VMEM((ITERS, piece, total // 2), F32),
            pltpu.VMEM((ITERS, piece, total // 2), F32),
            pltpu.VMEM((ITERS, half, piece, total // 2), F32),
            pltpu.VMEM((ITERS, 2, total, rows), F32),
            pltpu.VMEM((ITERS, 2, total, rows), F32),
            pltpu.VMEM((2, total, rows), F32),
            pltpu.VMEM((ITERS, 2, total, rows), F32),
            pltpu.VMEM((ITERS, 2, total, rows), F32),
            dma((4,)),
            dma((8, n)),
            dma((8, n)),
            dma((ITERS, 2, half)),
            dma((ITERS, 2, half)),
            dma((ITERS,)),
            dma((ITERS,)),
            dma((ITERS, 2, 2)),
            dma((ITERS, 2, 2)),
        ],
        compiler_params=pltpu.CompilerParams(
            collective_id=0, has_side_effects=True, vmem_limit_bytes=127 * 1024 * 1024 // 2
        ),
        cost_estimate=pl.CostEstimate(
            flops=ITERS * 4 * total * total * wl * (rows + 2 * OV),
            bytes_accessed=16 * c_loc * width * rows,
            transcendentals=0,
        ),
        name="denoise",
    )(cut(estimate), cut(dirty), cut(weights), margin, blend_table, tau_steps)
    return result.transpose(2, 0, 1, 3).reshape(c_loc, width, rows)


def solution(mesh):
    n, facets = mesh.shape["chan"], mesh.shape["facet"]
    cube = P("chan", None, "facet")
    return jax.shard_map(
        functools.partial(per_device, n, facets),
        mesh=mesh,
        in_specs=(cube, cube, cube, P(), P(), P()),
        out_specs=cube,
        check_vma=False,
    )
```
